128 devices in a mesh: row: 32 (over y, z_lo, x), col: 4 (over z_hi, core).
Axes of the slice: x: 4, y: 4, z: 4 (z_hi: 2, z_lo: 2; z = z_hi * 2 + z_lo), core: 2. Of those that a mesh axis runs over, the one named last changes fastest.
Arguments:
- pair_map: bfloat16 [1536, 1536, 128], P('row', 'col'), may hold values from -6 to 6
- valid_tokens: int32 [1536], replicated, may hold values from 0 to 1, as said below
- ln_gain: float32 [128], replicated, may hold values from 0.1 to 1.9
- ln_bias: float32 [128], replicated, may hold values from -3 to 3
- w_bias: bfloat16 [128, 4], replicated, may hold values from -0.5 to 0.5
- w_query: bfloat16 [128, 128], replicated, may hold values from -4.6 to 4.6
- w_key: bfloat16 [128, 128], replicated, may hold values from -4.6 to 4.6
- w_value: bfloat16 [128, 128], replicated, may hold values from -0.5 to 0.5
- w_gate: bfloat16 [128, 128], replicated, may hold values from -0.5 to 0.5
- gate_bias: float32 [128], replicated, may hold values from -4 to 4
- w_out: bfloat16 [128, 128], replicated, may hold values from -0.5 to 0.5
Outputs:
- update: bfloat16 [1536, 1536, 128], P('row', 'col')
The draws below stay inside these ranges and needn't reach their ends.
Inputs may be any that keep to these rules, and one draw needn't show every extreme that they name: `valid_tokens`: the residues form 4 chains of 384 positions each; in each chain the real residues come first, at least 192 of them, then padding.
All inputs are finite; a program needn't handle non-finite values.
Results may differ from the reference program's by a relative error of at most 0.014.
The reference program's roundings to bfloat16 on the way (of `normed`, `planes`, `weights` and `hidden`) count: a program that leaves them out, or rounds other values in their place, can miss the bound.
Values may be sent and summed in bfloat16 or wider, within the bound.
A program may use at most 256 MiB of HBM per device.

```python
import math
import jax
import jax.numpy as jnp
from jax import lax

D = 128
HEADS = 4
HEAD_DIM = 32
N = 1536


def draw_w_query(key, part):
    key = jax.random.fold_in(key, 5)
    own_part = jnp.clip(jax.random.normal(key, (D, HEADS * HEAD_DIM), jnp.float32), -6.0, 6.0)
    result = own_part / math.sqrt(D)
    return result.astype(jnp.bfloat16)


def draw_w_key(key, part):
    key = jax.random.fold_in(key, 7)
    own_part = jnp.clip(jax.random.normal(key, (D, HEADS * HEAD_DIM), jnp.float32), -6.0, 6.0)
    result = own_part / math.sqrt(D)
    return result.astype(jnp.bfloat16)


def draw_valid_tokens(key, part):
    key = jax.random.fold_in(key, 3)
    chain_len = N // 4
    lengths = jax.random.randint(key, (4,), chain_len // 2, chain_len + 1)
    positions = jnp.arange(N, dtype=jnp.int32)
    within = positions % chain_len
    chain_of = positions // chain_len
    limits = jnp.sum(jnp.where(chain_of[:, None] == jnp.arange(4, dtype=jnp.int32)[None, :], lengths[None, :], 0), axis=1)
    return (within < limits).astype(jnp.int32)


def levels(key, dims, split, low, top_value):
    gain, own = 1.0, jax.random.fold_in(key, 6)
    for dim, blocks in split:
        draws = jnp.exp(jax.random.uniform(jax.random.fold_in(own, dim), (blocks,), jnp.float32, low / len(split), top_value / len(split)))
        gain = gain * jnp.repeat(draws, dims[dim] // blocks).reshape([-1 if axis == dim else 1 for axis in range(len(dims))])
    return gain


def noise(key, extent, spread, limit, pieces=(), kind=jnp.bfloat16):
    values = spread * jax.random.normal(key, extent, jnp.float32)
    if pieces:
        values = values * levels(key, extent, pieces, -0.22, 0.18)
    return jnp.clip(values, -limit, limit).astype(kind)


def setup_inputs(seed: int = 0) -> dict:
    keys = jax.random.split(jax.random.key(seed), 12)
    return {
        "pair_map": noise(keys[0], (N, N, D), 1.0, 6.0, ((0, 32), (1, 4))),
        "valid_tokens": draw_valid_tokens(jax.random.fold_in(keys[11], 71), 0),
        "ln_gain": jnp.clip(1.0 + 0.18 * jax.random.normal(keys[2], (D,), jnp.float32), 0.1, 1.9),
        "ln_bias": noise(keys[3], (D,), 0.5, 3.0, (), jnp.float32),
        "w_bias": noise(keys[4], (D, HEADS), D ** -0.5, 0.5),
        "w_query": draw_w_query(jax.random.fold_in(keys[11], 71), 0),
        "w_key": draw_w_key(jax.random.fold_in(keys[11], 71), 0),
        "w_value": noise(keys[7], (D, HEADS * HEAD_DIM), D ** -0.5, 0.5),
        "w_gate": noise(keys[8], (D, HEADS * HEAD_DIM), D ** -0.5, 0.5),
        "gate_bias": noise(keys[9], (HEADS * HEAD_DIM,), 1.0, 4.0, (), jnp.float32),
        "w_out": noise(keys[10], (HEADS * HEAD_DIM, D), (HEADS * HEAD_DIM) ** -0.5, 0.5),
    }


def normalize(pair_map, ln_gain, ln_bias):
    values_f32 = pair_map.astype(jnp.float32)
    average = lax.optimization_barrier(jnp.mean(values_f32, axis=-1, keepdims=True))
    centered = values_f32 - average
    variance = lax.optimization_barrier(jnp.mean(centered * centered, axis=-1, keepdims=True))
    return (centered * lax.rsqrt(variance + 1e-05) * ln_gain + ln_bias).astype(jnp.bfloat16)

def reference(pair_map, valid_tokens, ln_gain, ln_bias, w_bias, w_query, w_key, w_value, w_gate, gate_bias, w_out):
    normed = normalize(pair_map, ln_gain, ln_bias)
    planes = jnp.dot(normed.reshape(N * N, D), w_bias, preferred_element_type=jnp.float32)
    planes = planes.astype(jnp.bfloat16).reshape(N, N, HEADS).transpose(2, 0, 1)
    planes_t = jnp.swapaxes(planes, 1, 2).astype(jnp.float32)
    negative = (valid_tokens.astype(jnp.float32) - 1.0) * 1000000000.0
    score_scale = 1.0 / math.sqrt(HEAD_DIM)
    columns = jnp.swapaxes(normed, 0, 1)

    def column(column_rows):
        query_col = (jnp.dot(column_rows, w_query, preferred_element_type=jnp.float32) * score_scale).astype(jnp.bfloat16)
        key_col = jnp.dot(column_rows, w_key, preferred_element_type=jnp.float32).astype(jnp.bfloat16)
        value_col = jnp.dot(column_rows, w_value, preferred_element_type=jnp.float32).astype(jnp.bfloat16)
        gate_value = jax.nn.sigmoid(jnp.dot(column_rows, w_gate, preferred_element_type=jnp.float32) + gate_bias)
        query_col = query_col.reshape(N, HEADS, HEAD_DIM).astype(jnp.float32)
        key_col = key_col.reshape(N, HEADS, HEAD_DIM).astype(jnp.float32)
        value_col = value_col.reshape(N, HEADS, HEAD_DIM).astype(jnp.float32)
        scores = jnp.einsum('ihc,khc->hik', query_col, key_col) + planes_t + negative
        weights = jax.nn.softmax(scores, axis=-1).astype(jnp.bfloat16)
        attended = jnp.einsum('hik,khc->ihc', weights.astype(jnp.float32), value_col)
        hidden = (gate_value * attended.reshape(N, HEADS * HEAD_DIM)).astype(jnp.bfloat16)
        return jnp.dot(hidden, w_out, preferred_element_type=jnp.float32).astype(jnp.bfloat16)
    updates = lax.map(column, columns)
    return jnp.swapaxes(updates, 0, 1)
```

```python
import functools
import math

import jax
import jax.numpy as jnp
from jax import lax
from jax.experimental import pallas as pl
from jax.experimental.pallas import tpu as pltpu
from jax.sharding import PartitionSpec as P

HEADS = 4
WIDTH = 32
GROUPS = 3
KEY_TILE = 256
LOG2E = 1.4426950408889634
F32 = jnp.float32
BF16 = jnp.bfloat16


def dot_nt(a, b):
    return lax.dot_general(a, b, (((1,), (1,)), ((), ())), preferred_element_type=F32)


def dot_tn(a, b):
    return lax.dot_general(a, b, (((0,), (0,)), ((), ())), preferred_element_type=F32)


def normalize_kernel(pair_ref, gain_ref, shift_ref, bias_ref, *out_refs):
    plane_ref, column_refs = out_refs[0], out_refs[1:]
    rows, cols, channels = pair_ref.shape
    owners, group_cols = column_refs[0].shape[:2]
    own_cols = group_cols * len(column_refs)
    gain, shift = gain_ref[...], shift_ref[...]
    for start in range(0, cols, own_cols * 4):
        width = own_cols * 4
        values = pair_ref[:, start : start + width, :].astype(F32)
        centered = values - jnp.mean(values, axis=-1, keepdims=True)
        variance = jnp.mean(centered * centered, axis=-1, keepdims=True)
        normed = centered * lax.rsqrt(variance + 1e-05) * gain + shift
        by_column = jnp.swapaxes(normed, 0, 1).astype(BF16)
        for owner in range(4):
            for group, ref in enumerate(column_refs):
                first = owner * own_cols + group * group_cols
                ref[start // own_cols + owner] = by_column[first : first + group_cols]
    for row in range(rows):
        values = pair_ref[row].astype(F32)
        centered = values - jnp.mean(values, axis=-1, keepdims=True)
        variance = jnp.mean(centered * centered, axis=-1, keepdims=True)
        normed = (centered * lax.rsqrt(variance + 1e-05) * gain + shift).astype(BF16)
        plane_ref[row] = dot_nt(bias_ref[...], normed)


def attend_kernel(
    order_ref, steps_ref, x_ref, planes_ref, valid_ref, wqg_ref, gate_bias_ref, wk_ref, wv_ref, wo_ref,
    out_ref, bias, keys, values, queries, summed, sems,
):
    blocks, _, block, channels = x_ref.shape
    length = blocks * block
    col_blocks = planes_ref.shape[1]
    col_width = planes_ref.shape[-1]
    steps = steps_ref[0]
    key_blocks = (steps * KEY_TILE + block - 1) // block

    def plane_copy(slot, col):
        return pltpu.make_async_copy(
            planes_ref.at[order_ref[slot], col],
            bias.at[:, pl.ds(pl.multiple_of(slot * block, block), block), pl.ds(col * col_width, col_width)],
            sems.at[0],
        )

    first = pl.program_id(0) == 0

    @pl.when(first)
    def _():
        @pl.loop(0, key_blocks)
        def _(slot):
            for col in range(col_blocks):
                plane_copy(slot, col).start()

    x = x_ref[...].reshape(length, channels)
    projected = dot_nt(wqg_ref[...], x)
    queries[...] = (projected[:channels] * (1.0 / math.sqrt(WIDTH))).astype(BF16)
    gate = jax.nn.sigmoid(projected[channels:] + gate_bias_ref[...])
    compact = jnp.concatenate([x_ref[order_ref[slot], 0] for slot in range(blocks)], axis=0)
    key_all = jnp.dot(compact, wk_ref[...], preferred_element_type=F32).astype(BF16)
    valid = valid_ref[...]
    value_all = (dot_nt(wv_ref[...], compact).astype(BF16).astype(F32) * valid[:1]).astype(BF16)
    ones = jnp.broadcast_to(valid[:1], (16, length)).astype(BF16)
    for head in range(HEADS):
        lanes = slice(head * WIDTH, (head + 1) * WIDTH)
        keys[head] = key_all[:, lanes]
        values[head, :WIDTH] = value_all[lanes]
        values[head, WIDTH:] = ones

    @pl.when(first)
    def _():
        @pl.loop(0, key_blocks)
        def _(slot):
            for col in range(col_blocks):
                plane_copy(slot, col).wait()

    def scores(head, at):
        heads = pl.ds(head * WIDTH, WIDTH)
        raw = jnp.dot(keys[head, at, :], queries[heads, :], preferred_element_type=F32)
        return raw + bias[head, at, :].astype(F32)

    def tile(step):
        return pl.ds(pl.multiple_of(step * KEY_TILE, KEY_TILE), KEY_TILE)

    summed[...] = jnp.zeros_like(summed)

    @pl.loop(0, steps)
    def _(step):
        at = tile(step)
        for head in range(HEADS):
            weights = jnp.exp(scores(head, at)).astype(BF16)
            summed[head] += jnp.dot(values[head, :, at], weights, preferred_element_type=F32)

    totals = summed[:, WIDTH, :]
    lowest, highest = jnp.min(totals), jnp.max(totals)
    safe = jnp.logical_and(lowest > 2.0**-60, highest < 2.0**100)

    @pl.when(jnp.logical_not(safe))
    def _():
        for head in range(HEADS):
            def masked(step):
                at = tile(step)
                real = jnp.transpose(valid_ref[:, at])[:, :1] > 0
                return at, jnp.where(real, scores(head, at), -3.0e38)

            def highest_of(step, top):
                return jnp.maximum(top, jnp.max(masked(step)[1], axis=0, keepdims=True))

            top = lax.fori_loop(0, steps, highest_of, jnp.full((1, length), -3.0e38, F32))
            summed[head] = jnp.zeros_like(summed[head])

            @pl.loop(0, steps)
            def _(step):
                at, shifted = masked(step)
                weights = jnp.exp(shifted - top).astype(BF16)
                summed[head] += jnp.dot(values[head, :, at], weights, preferred_element_type=F32)

    attended = jnp.concatenate(
        [summed[head, :WIDTH] / summed[head, WIDTH : WIDTH + 1] for head in range(HEADS)], axis=0
    )
    hidden = (gate * attended).astype(BF16)
    update = dot_tn(hidden, wo_ref[...]).astype(BF16)
    out_ref[...] = update.reshape(out_ref.shape)


def normalize(pair_map, ln_gain, ln_bias, w_bias, owners):
    rows, cols, channels = pair_map.shape
    own_cols = cols // owners
    group_cols = own_cols // GROUPS
    block = 16
    padded = jnp.zeros((8, channels), BF16).at[:HEADS].set(w_bias.T)
    group = jax.ShapeDtypeStruct((owners, group_cols, rows, channels), BF16)
    full = pl.BlockSpec((1, channels), lambda i: (0, 0))
    return pl.pallas_call(
        normalize_kernel,
        grid=(rows // block,),
        in_specs=[
            pl.BlockSpec((block, cols, channels), lambda i: (i, 0, 0)),
            full,
            full,
            pl.BlockSpec((8, channels), lambda i: (0, 0)),
        ],
        out_specs=[pl.BlockSpec((block, 8, cols), lambda i: (i, 0, 0))]
        + [pl.BlockSpec((owners, group_cols, block, channels), lambda i: (0, 0, i, 0))] * GROUPS,
        out_shape=[jax.ShapeDtypeStruct((rows, 8, cols), F32)] + [group] * GROUPS,
        compiler_params=pltpu.CompilerParams(vmem_limit_bytes=56 * 2**20),
        name="normalize",
    )(pair_map, ln_gain[None], ln_bias[None], padded)


def attend(x, planes, order, steps, valid, wqg, gate_bias, wk, wv, wo):
    blocks, cols, block, channels = x.shape
    length = blocks * block
    whole = lambda shape: pl.BlockSpec(shape, lambda j, *_: (0,) * len(shape))
    column = pl.BlockSpec((blocks, 1, block, channels), lambda j, *_: (0, j, 0, 0))
    scores = cols * HEADS * length * length
    return pl.pallas_call(
        attend_kernel,
        grid_spec=pltpu.PrefetchScalarGridSpec(
            num_scalar_prefetch=2,
            grid=(cols,),
            in_specs=[
                column,
                pl.BlockSpec(memory_space=pl.ANY),
                whole(valid.shape),
                whole(wqg.shape),
                whole(gate_bias.shape),
                whole(wk.shape),
                whole(wv.shape),
                whole(wo.shape),
            ],
            out_specs=column,
            scratch_shapes=[
                pltpu.VMEM((HEADS, length, length), BF16),
                pltpu.VMEM((HEADS, length, WIDTH), BF16),
                pltpu.VMEM((HEADS, WIDTH + 16, length), BF16),
                pltpu.VMEM((channels, length), BF16),
                pltpu.VMEM((HEADS, WIDTH + 16, length), F32),
                pltpu.SemaphoreType.DMA((1,)),
            ],
        ),
        out_shape=jax.ShapeDtypeStruct(x.shape, BF16),
        compiler_params=pltpu.CompilerParams(vmem_limit_bytes=60 * 2**20),
        cost_estimate=pl.CostEstimate(
            flops=scores * 512, bytes_accessed=planes.size * 2 + x.size * 4, transcendentals=scores
        ),
        name="attend",
    )(order, steps, x, planes, valid, wqg, gate_bias, wk, wv, wo)


def shards(
    pair_map, valid_tokens, ln_gain, ln_bias, w_bias, w_query, w_key, w_value, w_gate, gate_bias, w_out,
):
    rows, cols, channels = pair_map.shape
    owners = lax.axis_size("row")
    length = valid_tokens.shape[0]
    planes, *groups = normalize(pair_map, ln_gain, ln_bias, w_bias, owners)
    planes = jnp.swapaxes(planes[:, :HEADS], 0, 1).astype(BF16)
    received = [lax.all_to_all(group, "row", split_axis=0, concat_axis=0) for group in groups]
    planes = lax.all_gather(planes, "col")
    planes = lax.all_gather(planes, "row")

    blocks = valid_tokens.reshape(owners, rows)
    empty = jnp.max(blocks, axis=1) == 0
    order = jnp.argsort(empty, stable=True).astype(jnp.int32)
    filled = jnp.sum(jnp.logical_not(empty).astype(jnp.int32))
    steps = ((filled * rows + KEY_TILE - 1) // KEY_TILE).reshape(1).astype(jnp.int32)
    valid = jnp.broadcast_to(blocks[order].reshape(1, length).astype(F32), (8, length))
    wqg = jnp.concatenate([w_query, w_gate], axis=1).T
    arguments = (planes, order, steps, valid, wqg, gate_bias[:, None], w_key, w_value.T, w_out)
    returned = []
    for group in received:
        update = attend(group, *arguments)
        returned.append(lax.all_to_all(update, "row", split_axis=0, concat_axis=0))
    update = jnp.concatenate(returned, axis=1).reshape(cols, rows, channels)
    return jnp.swapaxes(update, 0, 1)


def solution(mesh):
    return jax.shard_map(
        shards,
        mesh=mesh,
        in_specs=(P("row", "col", None), P(), P(), P(), P(), P(), P(), P(), P(), P(), P()),
        out_specs=P("row", "col", None),
        check_vma=False,
    )
```

```python
import functools
import math

import jax
import jax.numpy as jnp
from jax import lax
from jax.experimental import pallas as pl
from jax.experimental.pallas import tpu as pltpu
from jax.sharding import PartitionSpec as P

HEADS = 4
WIDTH = 32
GROUPS = 3
KEY_TILE = 256
LOG2E = 1.4426950408889634
F32 = jnp.float32
BF16 = jnp.bfloat16


def dot_nt(a, b):
    return lax.dot_general(a, b, (((1,), (1,)), ((), ())), preferred_element_type=F32)


def dot_tn(a, b):
    return lax.dot_general(a, b, (((0,), (0,)), ((), ())), preferred_element_type=F32)


def normalize_kernel(pair_ref, gain_ref, shift_ref, bias_ref, *out_refs):
    plane_ref, column_refs = out_refs[0], out_refs[1:]
    rows, cols, channels = pair_ref.shape
    owners, group_cols = column_refs[0].shape[:2]
    own_cols = group_cols * len(column_refs)
    gain, shift = gain_ref[...], shift_ref[...]
    for start in range(0, cols, own_cols * 4):
        width = own_cols * 4
        values = pair_ref[:, start : start + width, :].astype(F32)
        centered = values - jnp.mean(values, axis=-1, keepdims=True)
        variance = jnp.mean(centered * centered, axis=-1, keepdims=True)
        normed = centered * lax.rsqrt(variance + 1e-05) * gain + shift
        by_column = jnp.swapaxes(normed, 0, 1).astype(BF16)
        for owner in range(4):
            for group, ref in enumerate(column_refs):
                first = owner * own_cols + group * group_cols
                ref[start // own_cols + owner] = by_column[first : first + group_cols]
    for row in range(rows):
        values = pair_ref[row].astype(F32)
        centered = values - jnp.mean(values, axis=-1, keepdims=True)
        variance = jnp.mean(centered * centered, axis=-1, keepdims=True)
        normed = (centered * lax.rsqrt(variance + 1e-05) * gain + shift).astype(BF16)
        plane_ref[row] = dot_nt(bias_ref[...], normed)


def attend_kernel(
    order_ref, steps_ref, x_ref, planes_ref, valid_ref, wqg_ref, gate_bias_ref, wk_ref, wv_ref, wo_ref,
    out_ref, bias, keys, values, queries, summed, sems,
):
    blocks, _, block, channels = x_ref.shape
    length = blocks * block
    col_blocks = 4
    col_width = planes_ref.shape[-1]
    steps = steps_ref[0]
    key_blocks = (steps * KEY_TILE + block - 1) // block

    def plane_copy(slot, col):
        row = order_ref[slot]
        return pltpu.make_async_copy(
            planes_ref.at[col % 2, row % 4, row // 8, col // 2 * 2 + row // 4 % 2],
            bias.at[:, pl.ds(pl.multiple_of(slot * block, block), block), pl.ds(col * col_width, col_width)],
            sems.at[0],
        )

    first = pl.program_id(0) == 0

    @pl.when(first)
    def _():
        @pl.loop(0, key_blocks)
        def _(slot):
            for col in range(col_blocks):
                plane_copy(slot, col).start()

    x = x_ref[...].reshape(length, channels)
    projected = dot_nt(wqg_ref[...], x)
    queries[...] = (projected[:channels] * (1.0 / math.sqrt(WIDTH))).astype(BF16)
    gate = jax.nn.sigmoid(projected[channels:] + gate_bias_ref[...])
    compact = jnp.concatenate([x_ref[order_ref[slot], 0] for slot in range(blocks)], axis=0)
    key_all = jnp.dot(compact, wk_ref[...], preferred_element_type=F32).astype(BF16)
    valid = valid_ref[...]
    value_all = (dot_nt(wv_ref[...], compact).astype(BF16).astype(F32) * valid[:1]).astype(BF16)
    ones = jnp.broadcast_to(valid[:1], (16, length)).astype(BF16)
    for head in range(HEADS):
        lanes = slice(head * WIDTH, (head + 1) * WIDTH)
        keys[head] = key_all[:, lanes]
        values[head, :WIDTH] = value_all[lanes]
        values[head, WIDTH:] = ones

    @pl.when(first)
    def _():
        @pl.loop(0, key_blocks)
        def _(slot):
            for col in range(col_blocks):
                plane_copy(slot, col).wait()

    def scores(head, at):
        heads = pl.ds(head * WIDTH, WIDTH)
        raw = jnp.dot(keys[head, at, :], queries[heads, :], preferred_element_type=F32)
        return raw + bias[head, at, :].astype(F32)

    def tile(step):
        return pl.ds(pl.multiple_of(step * KEY_TILE, KEY_TILE), KEY_TILE)

    summed[...] = jnp.zeros_like(summed)

    @pl.loop(0, steps)
    def _(step):
        at = tile(step)
        for head in range(HEADS):
            weights = jnp.exp(scores(head, at)).astype(BF16)
            summed[head] += jnp.dot(values[head, :, at], weights, preferred_element_type=F32)

    totals = summed[:, WIDTH, :]
    lowest, highest = jnp.min(totals), jnp.max(totals)
    safe = jnp.logical_and(lowest > 2.0**-60, highest < 2.0**100)

    @pl.when(jnp.logical_not(safe))
    def _():
        for head in range(HEADS):
            def masked(step):
                at = tile(step)
                real = jnp.transpose(valid_ref[:, at])[:, :1] > 0
                return at, jnp.where(real, scores(head, at), -3.0e38)

            def highest_of(step, top):
                return jnp.maximum(top, jnp.max(masked(step)[1], axis=0, keepdims=True))

            top = lax.fori_loop(0, steps, highest_of, jnp.full((1, length), -3.0e38, F32))
            summed[head] = jnp.zeros_like(summed[head])

            @pl.loop(0, steps)
            def _(step):
                at, shifted = masked(step)
                weights = jnp.exp(shifted - top).astype(BF16)
                summed[head] += jnp.dot(values[head, :, at], weights, preferred_element_type=F32)

    attended = jnp.concatenate(
        [summed[head, :WIDTH] / summed[head, WIDTH : WIDTH + 1] for head in range(HEADS)], axis=0
    )
    hidden = (gate * attended).astype(BF16)
    update = dot_tn(hidden, wo_ref[...]).astype(BF16)
    out_ref[...] = update.reshape(out_ref.shape)


def gather_kernel(own_ref, all_ref, own_sem, send_sems, recv_sems, pair_send, pair_recv):
    row, col = lax.axis_index("row"), lax.axis_index("col")
    core = col % 2
    here = {"x": row % 4, "y": row // 8, "z": col // 2 * 2 + row // 4 % 2}

    def device(place, on_core):
        return ((place["y"] * 2 + place["z"] % 2) * 4 + place["x"], place["z"] // 2 * 2 + on_core)

    def moved(axis, by):
        return {**here, axis: (here[axis] + by) % 4}

    partner = device(here, 1 - core)
    barrier = pltpu.get_barrier_semaphore()
    friends = [device(moved(axis, by), core) for axis in "xyz" for by in (1, 3)] + [partner]
    for friend in friends:
        pl.semaphore_signal(barrier, inc=1, device_id=friend, device_id_type=pl.DeviceIdType.MESH)
    pl.semaphore_wait(barrier, len(friends))

    mine = pltpu.make_async_copy(own_ref, all_ref.at[core, here["x"], here["y"], here["z"]], own_sem)
    mine.start()
    mine.wait()
    orders = ("zyx", "xzy", "yxz")

    def region(part, stage, by, heads):
        place = []
        for axis in "xyz":
            at = orders[part].index(axis)
            if at < stage:
                place.append(slice(None))
            elif at == stage:
                place.append((here[axis] + by) % 4)
            else:
                place.append(here[axis])
        return all_ref.at[(core, *place, heads, pl.ds(part * 16, 16))]

    every, low, high = slice(None), pl.ds(0, 2), pl.ds(2, 2)

    def send(part, stage, kind, by, heads, to):
        ref = region(part, stage, by, heads)
        copy = pltpu.make_async_remote_copy(
            src_ref=ref,
            dst_ref=ref,
            send_sem=send_sems.at[part, stage, kind],
            recv_sem=recv_sems.at[part, stage, kind],
            device_id=device(moved(orders[part][stage], to), core),
            device_id_type=pl.DeviceIdType.MESH,
        )
        copy.start()
        return copy

    def pair(part, piece, by):
        ref = region(part, 2, by, every)
        copy = pltpu.make_async_remote_copy(
            src_ref=ref,
            dst_ref=ref,
            send_sem=pair_send.at[part, piece],
            recv_sem=pair_recv.at[part, piece],
            device_id=partner,
            device_id_type=pl.DeviceIdType.MESH,
        )
        copy.start()
        return copy

    copies, pairs = [], []
    for stage in range(3):
        last = stage == 2
        near = []
        for part in range(3):
            near.append((send(part, stage, 0, 0, every, 1), send(part, stage, 1, 0, every, 3)))
            if last:
                pairs.append(pair(part, 0, 0))
        far = []
        for part in range(3):
            near[part][0].wait_recv()
            near[part][1].wait_recv()
            far.append((send(part, stage, 2, 3, low, 1), send(part, stage, 3, 1, high, 3)))
            if last:
                pairs += [pair(part, 1, 3), pair(part, 2, 1)]
        for part in range(3):
            far[part][0].wait_recv()
            far[part][1].wait_recv()
            if last:
                pairs.append(pair(part, 3, 2))
        copies += [copy for two in near + far for copy in two]
    for copy in copies:
        copy.wait_send()
    for copy in pairs:
        copy.wait()


def gather(planes):
    heads, rows, cols = planes.shape
    return pl.pallas_call(
        gather_kernel,
        in_specs=[pl.BlockSpec(memory_space=pl.ANY)],
        out_specs=pl.BlockSpec(memory_space=pl.ANY),
        out_shape=jax.ShapeDtypeStruct((2, 4, 4, 4, heads, rows, cols), BF16),
        scratch_shapes=[
            pltpu.SemaphoreType.DMA,
            pltpu.SemaphoreType.DMA((3, 3, 4)),
            pltpu.SemaphoreType.DMA((3, 3, 4)),
            pltpu.SemaphoreType.DMA((3, 4)),
            pltpu.SemaphoreType.DMA((3, 4)),
        ],
        compiler_params=pltpu.CompilerParams(collective_id=0, has_side_effects=True),
        name="gather_planes",
    )(planes)


def normalize(pair_map, ln_gain, ln_bias, w_bias, owners):
    rows, cols, channels = pair_map.shape
    own_cols = cols // owners
    group_cols = own_cols // GROUPS
    block = 16
    padded = jnp.zeros((8, channels), BF16).at[:HEADS].set(w_bias.T)
    group = jax.ShapeDtypeStruct((owners, group_cols, rows, channels), BF16)
    full = pl.BlockSpec((1, channels), lambda i: (0, 0))
    return pl.pallas_call(
        normalize_kernel,
        grid=(rows // block,),
        in_specs=[
            pl.BlockSpec((block, cols, channels), lambda i: (i, 0, 0)),
            full,
            full,
            pl.BlockSpec((8, channels), lambda i: (0, 0)),
        ],
        out_specs=[pl.BlockSpec((block, 8, cols), lambda i: (i, 0, 0))]
        + [pl.BlockSpec((owners, group_cols, block, channels), lambda i: (0, 0, i, 0))] * GROUPS,
        out_shape=[jax.ShapeDtypeStruct((rows, 8, cols), F32)] + [group] * GROUPS,
        compiler_params=pltpu.CompilerParams(vmem_limit_bytes=56 * 2**20),
        name="normalize",
    )(pair_map, ln_gain[None], ln_bias[None], padded)


def attend(x, planes, order, steps, valid, wqg, gate_bias, wk, wv, wo):
    blocks, cols, block, channels = x.shape
    length = blocks * block
    whole = lambda shape: pl.BlockSpec(shape, lambda j, *_: (0,) * len(shape))
    column = pl.BlockSpec((blocks, 1, block, channels), lambda j, *_: (0, j, 0, 0))
    scores = cols * HEADS * length * length
    return pl.pallas_call(
        attend_kernel,
        grid_spec=pltpu.PrefetchScalarGridSpec(
            num_scalar_prefetch=2,
            grid=(cols,),
            in_specs=[
                column,
                pl.BlockSpec(memory_space=pl.ANY),
                whole(valid.shape),
                whole(wqg.shape),
                whole(gate_bias.shape),
                whole(wk.shape),
                whole(wv.shape),
                whole(wo.shape),
            ],
            out_specs=column,
            scratch_shapes=[
                pltpu.VMEM((HEADS, length, length), BF16),
                pltpu.VMEM((HEADS, length, WIDTH), BF16),
                pltpu.VMEM((HEADS, WIDTH + 16, length), BF16),
                pltpu.VMEM((channels, length), BF16),
                pltpu.VMEM((HEADS, WIDTH + 16, length), F32),
                pltpu.SemaphoreType.DMA((1,)),
            ],
        ),
        out_shape=jax.ShapeDtypeStruct(x.shape, BF16),
        compiler_params=pltpu.CompilerParams(vmem_limit_bytes=60 * 2**20),
        cost_estimate=pl.CostEstimate(
            flops=scores * 512, bytes_accessed=planes.size * 2 + x.size * 4, transcendentals=scores
        ),
        name="attend",
    )(order, steps, x, planes, valid, wqg, gate_bias, wk, wv, wo)


def shards(
    pair_map, valid_tokens, ln_gain, ln_bias, w_bias, w_query, w_key, w_value, w_gate, gate_bias, w_out,
):
    rows, cols, channels = pair_map.shape
    owners = lax.axis_size("row")
    length = valid_tokens.shape[0]
    planes, *groups = normalize(pair_map, ln_gain, ln_bias, w_bias, owners)
    planes = jnp.swapaxes(planes[:, :HEADS], 0, 1).astype(BF16)
    received = [lax.all_to_all(group, "row", split_axis=0, concat_axis=0) for group in groups]
    planes = gather(planes)

    blocks = valid_tokens.reshape(owners, rows)
    empty = jnp.max(blocks, axis=1) == 0
    order = jnp.argsort(empty, stable=True).astype(jnp.int32)
    filled = jnp.sum(jnp.logical_not(empty).astype(jnp.int32))
    steps = ((filled * rows + KEY_TILE - 1) // KEY_TILE).reshape(1).astype(jnp.int32)
    valid = jnp.broadcast_to(blocks[order].reshape(1, length).astype(F32), (8, length))
    wqg = jnp.concatenate([w_query, w_gate], axis=1).T
    arguments = (planes, order, steps, valid, wqg, gate_bias[:, None], w_key, w_value.T, w_out)
    returned = []
    for group in received:
        update = attend(group, *arguments)
        returned.append(lax.all_to_all(update, "row", split_axis=0, concat_axis=0))
    update = jnp.concatenate(returned, axis=1).reshape(cols, rows, channels)
    return jnp.swapaxes(update, 0, 1)


def solution(mesh):
    return jax.shard_map(
        shards,
        mesh=mesh,
        in_specs=(P("row", "col", None), P(), P(), P(), P(), P(), P(), P(), P(), P(), P()),
        out_specs=P("row", "col", None),
        check_vma=False,
    )
```

```python
import math

import jax
import jax.numpy as jnp
from jax import lax
from jax.experimental import pallas as pl
from jax.experimental.pallas import tpu as pltpu
from jax.sharding import PartitionSpec as P

HEADS = 4
WIDTH = 32
SPLIT = (4, 5, 3)
UNIT = 16
F32 = jnp.float32
BF16 = jnp.bfloat16


def dot_nt(a, b):
    return lax.dot_general(a, b, (((1,), (1,)), ((), ())), preferred_element_type=F32)


def dot_tn(a, b):
    return lax.dot_general(a, b, (((0,), (0,)), ((), ())), preferred_element_type=F32)


def turned(matrix):
    return jnp.transpose(matrix.astype(F32)).astype(BF16)


def begin_kernel(
    pair_hbm, gain_ref, shift_ref, bias_ref, all_ref, first_ref, later_ref,
    pair_ref, columns, planes, in_sems, own_sems, late_sems, send_sems, recv_sems,
    pair_send, pair_recv, block_send, block_recv,
):
    rows, cols, channels = pair_ref.shape
    owners = first_ref.shape[0]
    own_cols = cols // owners
    row, col = lax.axis_index("row"), lax.axis_index("col")
    core = col % 2
    here = {"x": row % 4, "y": row // 8, "z": col // 2 * 2 + row // 4 % 2}
    mesh_ids = pl.DeviceIdType.MESH

    def device(place, on_core):
        return ((place["y"] * 2 + place["z"] % 2) * 4 + place["x"], place["z"] // 2 * 2 + on_core)

    def moved(axis, by):
        return {**here, axis: (here[axis] + by) % 4}

    part_rows = rows // 3
    loads = []
    for part in range(3):
        at_rows = pl.ds(part * part_rows, part_rows)
        copy = pltpu.make_async_copy(pair_hbm.at[at_rows], pair_ref.at[at_rows], in_sems.at[part])
        copy.start()
        loads.append(copy)
    partner = device(here, 1 - core)
    outside = device(moved("z", 3 + 2 * (here["z"] % 2)), core)
    peers = [((row + step) % owners, col) for step in range(1, owners)]
    barrier = pltpu.get_barrier_semaphore()
    for friend in peers + [partner, outside]:
        pl.semaphore_signal(barrier, inc=1, device_id=friend, device_id_type=mesh_ids)

    orders = ("zyx", "xzy", "yxz")
    every, low, high = slice(None), pl.ds(0, 2), pl.ds(2, 2)

    def region(part, stage, by, heads):
        place = {}
        for axis in "xyz":
            at = orders[part].index(axis)
            place[axis] = None if at < stage else (here[axis] + by) % 4 if at == stage else here[axis]
        pick = lambda value: slice(None) if value is None else value
        z = place["z"]
        z_hi, z_lo = (None, None) if z is None else (z // 2, z % 2)
        index = (pick(z_hi), core, pick(place["x"]), pick(place["y"]), pick(z_lo), heads)
        return all_ref.at[(*index, pl.ds(part * part_rows, part_rows))]

    def remote(src, dst, sends, recvs, to):
        copy = pltpu.make_async_remote_copy(
            src_ref=src, dst_ref=dst, send_sem=sends, recv_sem=recvs, device_id=to, device_id_type=mesh_ids
        )
        copy.start()
        return copy

    def send(part, stage, kind, by, heads, to):
        ref = region(part, stage, by, heads)
        src = planes.at[:, pl.ds(part * part_rows, part_rows)] if stage == 0 and kind < 2 else ref
        sems = (send_sems.at[part, stage, kind], recv_sems.at[part, stage, kind])
        return remote(src, ref, *sems, device(moved(orders[part][stage], to), core))

    def pair(part, piece, by):
        ref = region(part, 2, by, every)
        return remote(ref, ref, pair_send.at[part, piece], pair_recv.at[part, piece], partner)

    gain, shift = gain_ref[...], shift_ref[...]
    to_planes = turned(jnp.concatenate([bias_ref[...], jnp.zeros((channels, channels - HEADS), BF16)], axis=1))[:8]
    width = 128
    mine, near = [], []
    for part in range(3):
        at_rows = slice(part * part_rows, (part + 1) * part_rows)
        loads[part].wait()

        @pl.loop(0, cols // width)
        def _(chunk):
            at_cols = pl.ds(pl.multiple_of(chunk * width, width), width)
            values = pair_ref[at_rows, at_cols, :].astype(F32)
            centered = values - jnp.mean(values, axis=-1, keepdims=True)
            variance = jnp.mean(centered * centered, axis=-1, keepdims=True)
            normed = centered * lax.rsqrt(variance + 1e-05) * gain + shift
            columns[at_cols, at_rows, :] = jnp.swapaxes(normed, 0, 1).astype(BF16)
            flat = normed.astype(BF16).reshape(part_rows * width, channels)
            by_row = dot_nt(to_planes, flat)
            stacked = jnp.stack([by_row[:, r * width : (r + 1) * width] for r in range(part_rows)], axis=0)
            planes[:, at_rows, at_cols] = jnp.swapaxes(stacked, 0, 1)[:HEADS].astype(BF16)

        if part == 0:
            pl.semaphore_wait(barrier, len(peers) + 2)
        copy = pltpu.make_async_copy(planes.at[:, at_rows], region(part, 0, 0, every), own_sems.at[part])
        copy.start()
        mine.append(copy)
        near.append((send(part, 0, 0, 0, every, 1), send(part, 0, 1, 0, every, 3)))

    first_cols = first_ref.shape[1]
    blocks = []
    for step in range(1, owners):
        to = (row + step) % owners
        src = columns.at[pl.ds(to * own_cols, first_cols)]
        blocks.append(remote(src, first_ref.at[row], block_send.at[step], block_recv.at[step], (to, col)))
    copy = pltpu.make_async_copy(
        columns.at[pl.ds(row * own_cols, first_cols)], first_ref.at[row], own_sems.at[3]
    )
    copy.start()
    mine.append(copy)
    for owner in range(owners):
        src = columns.at[pl.ds(owner * own_cols + first_cols, own_cols - first_cols)]
        copy = pltpu.make_async_copy(src, later_ref.at[owner], late_sems.at[owner])
        copy.start()
        mine.append(copy)
    for copy in mine[:3]:
        copy.wait()

    copies, pairs = [], []
    for stage in range(3):
        last = stage == 2
        if stage:
            near = []
            for part in range(3):
                near.append((send(part, stage, 0, 0, every, 1), send(part, stage, 1, 0, every, 3)))
                if last:
                    pairs.append(pair(part, 0, 0))
        far = []
        for part in range(3):
            near[part][0].wait_recv()
            near[part][1].wait_recv()
            far.append((send(part, stage, 2, 3, low, 1), send(part, stage, 3, 1, high, 3)))
            if last:
                pairs += [pair(part, 1, 3), pair(part, 2, 1)]
        for part in range(3):
            far[part][0].wait_recv()
            far[part][1].wait_recv()
            if last:
                pairs.append(pair(part, 3, 2))
        copies += [copy for two in near + far for copy in two]
    for copy in copies:
        copy.wait_send()
    for copy in pairs + blocks + mine[3:]:
        copy.wait()


def begin(pair_map, ln_gain, ln_bias, w_bias, owners):
    rows, cols, channels = pair_map.shape
    counts = (SPLIT[0], sum(SPLIT[1:]))
    groups = [jax.ShapeDtypeStruct((owners, count, rows, channels), BF16) for count in counts]
    planes = jax.ShapeDtypeStruct((2, 2, 4, 4, 2, HEADS, rows, cols), BF16)
    vmem, anywhere = pl.BlockSpec(memory_space=pltpu.VMEM), pl.BlockSpec(memory_space=pl.ANY)
    dma = pltpu.SemaphoreType.DMA
    return pl.pallas_call(
        begin_kernel,
        in_specs=[anywhere] + [vmem] * 3,
        out_specs=[anywhere] * 3,
        out_shape=[planes] + groups,
        scratch_shapes=[
            pltpu.VMEM((rows, cols, channels), BF16),
            pltpu.VMEM((cols, rows, channels), BF16),
            pltpu.VMEM((HEADS, rows, cols), BF16),
            dma((3,)),
            dma((4,)),
            dma((owners,)),
            dma((3, 3, 4)),
            dma((3, 3, 4)),
            dma((3, 4)),
            dma((3, 4)),
            dma((owners,)),
            dma((owners,)),
        ],
        compiler_params=pltpu.CompilerParams(
            collective_id=0, has_side_effects=True, vmem_limit_bytes=60 * 2**20
        ),
        name="begin",
    )(pair_map, ln_gain[None], ln_bias[None], w_bias)


def give_back_kernel(mine_ref, got_ref, own_sem, sends, recvs):
    owners = mine_ref.shape[0]
    row, col = lax.axis_index("row"), lax.axis_index("col")
    barrier = pltpu.get_barrier_semaphore()
    peers = [(row + step) % owners for step in range(1, owners)]
    for peer in peers:
        pl.semaphore_signal(barrier, inc=1, device_id=(peer, col), device_id_type=pl.DeviceIdType.MESH)
    own = pltpu.make_async_copy(mine_ref.at[row], got_ref.at[row], own_sem)
    own.start()
    pl.semaphore_wait(barrier, len(peers))
    copies = []
    for step, peer in enumerate(peers):
        copy = pltpu.make_async_remote_copy(
            src_ref=mine_ref.at[peer],
            dst_ref=got_ref.at[row],
            send_sem=sends.at[step],
            recv_sem=recvs.at[step],
            device_id=(peer, col),
            device_id_type=pl.DeviceIdType.MESH,
        )
        copy.start()
        copies.append(copy)
    own.wait()
    for copy in copies:
        copy.wait()


def give_back(update):
    owners = update.shape[0]
    return pl.pallas_call(
        give_back_kernel,
        in_specs=[pl.BlockSpec(memory_space=pl.ANY)],
        out_specs=pl.BlockSpec(memory_space=pl.ANY),
        out_shape=jax.ShapeDtypeStruct(update.shape, BF16),
        scratch_shapes=[
            pltpu.SemaphoreType.DMA,
            pltpu.SemaphoreType.DMA((owners - 1,)),
            pltpu.SemaphoreType.DMA((owners - 1,)),
        ],
        compiler_params=pltpu.CompilerParams(collective_id=1, has_side_effects=True),
        name="give_back",
    )(update)


def attend_kernel(
    tokens_ref, x_ref, planes_ref, real_ref, wq_ref, wk_ref, wv_ref, wg_ref, gate_bias_ref, wo_ref,
    out_ref, bias, keys, values, queries, summed, real, wqg, wv, gate_bias, order, sems,
):
    owners, _, rows, channels = x_ref.shape
    length = owners * rows
    units, per_owner = length // UNIT, rows // UNIT
    chain_units = units // 4
    first = pl.program_id(0) == 0

    def filled(chain):
        def count(unit, total):
            return total + tokens_ref[(chain * chain_units + unit) * UNIT]

        return lax.fori_loop(0, chain_units, count, jnp.int32(0))

    @pl.when(first)
    def _():
        ends = jnp.int32(0)
        for chain in range(4):
            here = filled(chain)

            def note(unit, start, chain=chain):
                order[start + unit] = chain * chain_units + unit
                return start

            lax.fori_loop(0, here, note, ends)
            ends = ends + here
        order[units] = ends

        @pl.loop(ends, units)
        def _(unit):
            order[unit] = 0

    count = order[units]
    tiles = (count + 7) // 8

    def plane_copy(slot):
        unit = order[slot]
        owner = unit // per_owner
        at = pl.ds(pl.multiple_of(unit % per_owner * UNIT, UNIT), UNIT)
        to = pl.ds(pl.multiple_of(slot * UNIT, UNIT), UNIT)
        return pltpu.make_async_copy(
            planes_ref.at[:, :, owner % 4, owner // 8, owner // 4 % 2, :, at, :],
            bias.at[:, :, :, to, :],
            sems.at[slot // 16],
        )

    @pl.when(first)
    def _():
        @pl.loop(0, tiles * 8)
        def _(slot):
            plane_copy(slot).start()

        for slot in range(units):
            unit = order[slot]
            at = pl.ds(pl.multiple_of(unit * UNIT, UNIT), UNIT)
            keep = jnp.where(slot < count, 1.0, 0.0).astype(F32)
            real[slot * UNIT : (slot + 1) * UNIT, :] = (real_ref[at, :].astype(F32) * keep).astype(BF16)
        wqg[:channels] = turned(wq_ref[...])
        wqg[channels:] = turned(wg_ref[...])
        wv[...] = turned(wv_ref[...])
        gate_bias[...] = jnp.transpose(jnp.broadcast_to(gate_bias_ref[...], (channels, channels)))

    x = x_ref[...].reshape(length, channels)
    projected = dot_nt(wqg[...], x)
    queries[...] = (projected[:channels] * (1.0 / math.sqrt(WIDTH))).astype(BF16)
    gate = jax.nn.sigmoid(projected[channels:] + gate_bias[:, :1])
    pieces = []
    for slot in range(units):
        unit = order[slot]
        at = pl.ds(pl.multiple_of(unit % per_owner * UNIT, UNIT), UNIT)
        pieces.append(x_ref[unit // per_owner, 0, at, :])
    compact = jnp.concatenate(pieces, axis=0) * real[...]
    key_all = jnp.dot(compact, wk_ref[...], preferred_element_type=F32).astype(BF16)
    value_all = dot_nt(wv[...], compact).astype(BF16)
    ones = dot_nt(jnp.full((16, channels), 1.0 / channels, BF16), real[...]).astype(BF16)
    for head in range(HEADS):
        lanes = slice(head * WIDTH, (head + 1) * WIDTH)
        keys[head] = key_all[:, lanes]
        values[head, :WIDTH] = value_all[lanes]
        values[head, WIDTH:] = ones

    def arrived(start, count):
        @pl.when(first)
        def _():
            @pl.loop(start, start + count)
            def _(slot):
                plane_copy(slot).wait()

    def scores(head, at):
        heads = pl.ds(head * WIDTH, WIDTH)
        raw = jnp.dot(keys[head, at, :], queries[heads, :], preferred_element_type=F32)
        added = [bias[z, core, head, at, :] for z in range(2) for core in range(2)]
        return raw + jnp.concatenate(added, axis=1).astype(F32)

    summed[...] = jnp.zeros_like(summed)

    def advance(at):
        for head in range(HEADS):
            weights = jnp.exp(scores(head, at)).astype(BF16)
            summed[head] += jnp.dot(values[head, :, at], weights, preferred_element_type=F32)

    wide = tiles // 2

    @pl.loop(0, wide)
    def _(step):
        arrived(step * 16, 16)
        advance(pl.ds(pl.multiple_of(step * 256, 256), 256))

    @pl.when(tiles % 2 == 1)
    def _():
        arrived(wide * 16, 8)
        advance(pl.ds(pl.multiple_of(wide * 256, 256), 128))

    totals = summed[:, WIDTH, :]
    lowest, highest = jnp.min(totals), jnp.max(totals)
    safe = jnp.logical_and(lowest > 2.0**-60, highest < 2.0**100)

    @pl.when(jnp.logical_not(safe))
    def _():
        for head in range(HEADS):

            def masked(step):
                at = pl.ds(pl.multiple_of(step * 128, 128), 128)
                return at, jnp.where(real[at, :1].astype(F32) > 0, scores(head, at), -3.0e38)

            def highest_of(step, top):
                return jnp.maximum(top, jnp.max(masked(step)[1], axis=0, keepdims=True))

            top = lax.fori_loop(0, tiles, highest_of, jnp.full((1, length), -3.0e38, F32))
            summed[head] = jnp.zeros_like(summed[head])

            @pl.loop(0, tiles)
            def _(step):
                at, shifted = masked(step)
                weights = jnp.exp(shifted - top).astype(BF16)
                summed[head] += jnp.dot(values[head, :, at], weights, preferred_element_type=F32)

    attended = jnp.concatenate(
        [summed[head, :WIDTH] / summed[head, WIDTH : WIDTH + 1] for head in range(HEADS)], axis=0
    )
    hidden = (gate * attended).astype(BF16)
    update = dot_tn(hidden, wo_ref[...]).astype(BF16)
    out_ref[...] = update.reshape(out_ref.shape)


def attend(x, start, cols, planes, tokens, real, wq, wk, wv, wg, gate_bias, wo):
    owners, _, rows, channels = x.shape
    length = owners * rows
    whole = lambda shape: pl.BlockSpec(shape, lambda j, *_: (0,) * len(shape))
    column = pl.BlockSpec((owners, 1, rows, channels), lambda j, *_: (0, j + start, 0, 0))
    result = pl.BlockSpec((owners, 1, rows, channels), lambda j, *_: (0, j, 0, 0))
    scores = cols * HEADS * length * length
    return pl.pallas_call(
        attend_kernel,
        grid_spec=pltpu.PrefetchScalarGridSpec(
            num_scalar_prefetch=1,
            grid=(cols,),
            in_specs=[
                column,
                pl.BlockSpec(memory_space=pl.ANY),
                whole(real.shape),
                whole(wq.shape),
                whole(wk.shape),
                whole(wv.shape),
                whole(wg.shape),
                whole(gate_bias.shape),
                whole(wo.shape),
            ],
            out_specs=result,
            scratch_shapes=[
                pltpu.VMEM((2, 2, HEADS, length, length // 4), BF16),
                pltpu.VMEM((HEADS, length, WIDTH), BF16),
                pltpu.VMEM((HEADS, WIDTH + 16, length), BF16),
                pltpu.VMEM((channels, length), BF16),
                pltpu.VMEM((HEADS, WIDTH + 16, length), F32),
                pltpu.VMEM((length, channels), BF16),
                pltpu.VMEM((2 * channels, channels), BF16),
                pltpu.VMEM((channels, channels), BF16),
                pltpu.VMEM((channels, channels), F32),
                pltpu.SMEM((length // UNIT + 1,), jnp.int32),
                pltpu.SemaphoreType.DMA((length // (16 * UNIT),)),
            ],
        ),
        out_shape=jax.ShapeDtypeStruct((owners, cols, rows, channels), BF16),
        compiler_params=pltpu.CompilerParams(vmem_limit_bytes=60 * 2**20),
        cost_estimate=pl.CostEstimate(
            flops=scores * 2048, bytes_accessed=planes.size * 2 + x.size * 4, transcendentals=scores
        ),
        name="attend",
    )(tokens, x, planes, real, wq, wk, wv, wg, gate_bias, wo)


def shards(
    pair_map, valid_tokens, ln_gain, ln_bias, w_bias, w_query, w_key, w_value, w_gate, gate_bias, w_out,
):
    rows, cols, channels = pair_map.shape
    owners = lax.axis_size("row")
    length = valid_tokens.shape[0]
    planes, first, later = begin(pair_map, ln_gain, ln_bias, w_bias, owners)
    later = lax.all_to_all(later, "row", split_axis=0, concat_axis=0)
    real = jnp.broadcast_to(valid_tokens[:, None], (length, channels)).astype(BF16)
    arguments = (planes, valid_tokens, real, w_query, w_key, w_value, w_gate, gate_bias[None], w_out)
    returned = []
    source, start = first, 0
    for index, count in enumerate(SPLIT):
        update = attend(source, start, count, *arguments)
        start = start + count if index else 0
        source = later
        if index < len(SPLIT) - 1:
            returned.append(lax.all_to_all(update, "row", split_axis=0, concat_axis=0))
        else:
            returned.append(give_back(update))
    update = jnp.concatenate(returned, axis=1).reshape(cols, rows, channels)
    return jnp.swapaxes(update, 0, 1)


def solution(mesh):
    return jax.shard_map(
        shards,
        mesh=mesh,
        in_specs=(P("row", "col", None), P(), P(), P(), P(), P(), P(), P(), P(), P(), P()),
        out_specs=P("row", "col", None),
        check_vma=False,
    )
```

```python
import math

import jax
import jax.numpy as jnp
from jax import lax
from jax.experimental import pallas as pl
from jax.experimental.pallas import tpu as pltpu
from jax.sharding import PartitionSpec as P

HEADS = 4
WIDTH = 32
SPLIT = (4, 5, 3)
UNIT = 16
F32 = jnp.float32
BF16 = jnp.bfloat16


def dot_nt(a, b):
    return lax.dot_general(a, b, (((1,), (1,)), ((), ())), preferred_element_type=F32)


def dot_tn(a, b):
    return lax.dot_general(a, b, (((0,), (0,)), ((), ())), preferred_element_type=F32)


def turned(matrix):
    return jnp.transpose(matrix.astype(F32)).astype(BF16)


def begin_kernel(
    pair_hbm, gain_ref, shift_ref, bias_ref, all_ref, first_ref, later_ref,
    pair_ref, columns, planes, in_sems, own_sems, late_sems, send_sems, recv_sems,
    pair_send, pair_recv, block_send, block_recv,
):
    rows, cols, channels = pair_ref.shape
    owners = first_ref.shape[0]
    own_cols = cols // owners
    row, col = lax.axis_index("row"), lax.axis_index("col")
    core = col % 2
    here = {"x": row % 4, "y": row // 8, "z": col // 2 * 2 + row // 4 % 2}
    mesh_ids = pl.DeviceIdType.MESH

    def device(place, on_core):
        return ((place["y"] * 2 + place["z"] % 2) * 4 + place["x"], place["z"] // 2 * 2 + on_core)

    def moved(axis, by):
        return {**here, axis: (here[axis] + by) % 4}

    part_rows = rows // 3
    loads = []
    for part in range(3):
        at_rows = pl.ds(part * part_rows, part_rows)
        copy = pltpu.make_async_copy(pair_hbm.at[at_rows], pair_ref.at[at_rows], in_sems.at[part])
        copy.start()
        loads.append(copy)
    partner = device(here, 1 - core)
    outside = device(moved("z", 3 + 2 * (here["z"] % 2)), core)
    peers = [((row + step) % owners, col) for step in range(1, owners)]
    barrier = pltpu.get_barrier_semaphore()
    for friend in peers + [partner, outside]:
        pl.semaphore_signal(barrier, inc=1, device_id=friend, device_id_type=mesh_ids)

    orders = ("zyx", "xzy", "yxz")
    every, low, high = slice(None), pl.ds(0, 2), pl.ds(2, 2)

    def region(part, stage, by, heads):
        place = {}
        for axis in "xyz":
            at = orders[part].index(axis)
            place[axis] = None if at < stage else (here[axis] + by) % 4 if at == stage else here[axis]
        pick = lambda value: slice(None) if value is None else value
        z = place["z"]
        z_hi, z_lo = (None, None) if z is None else (z // 2, z % 2)
        index = (pick(z_hi), core, pick(place["x"]), pick(place["y"]), pick(z_lo), heads)
        return all_ref.at[(*index, pl.ds(part * part_rows, part_rows))]

    def remote(src, dst, sends, recvs, to):
        copy = pltpu.make_async_remote_copy(
            src_ref=src, dst_ref=dst, send_sem=sends, recv_sem=recvs, device_id=to, device_id_type=mesh_ids
        )
        copy.start()
        return copy

    def send(part, stage, kind, by, heads, to):
        ref = region(part, stage, by, heads)
        src = planes.at[:, pl.ds(part * part_rows, part_rows)] if stage == 0 and kind < 2 else ref
        sems = (send_sems.at[part, stage, kind], recv_sems.at[part, stage, kind])
        return remote(src, ref, *sems, device(moved(orders[part][stage], to), core))

    def pair(part, piece, by):
        ref = region(part, 2, by, every)
        return remote(ref, ref, pair_send.at[part, piece], pair_recv.at[part, piece], partner)

    gain, shift = gain_ref[...], shift_ref[...]
    to_planes = turned(jnp.concatenate([bias_ref[...], jnp.zeros((channels, channels - HEADS), BF16)], axis=1))[:8]
    width = 128
    mine, near = [], []
    for part in range(3):
        at_rows = slice(part * part_rows, (part + 1) * part_rows)
        loads[part].wait()

        @pl.loop(0, cols // width)
        def _(chunk):
            at_cols = pl.ds(pl.multiple_of(chunk * width, width), width)
            values = pair_ref[at_rows, at_cols, :].astype(F32)
            centered = values - jnp.mean(values, axis=-1, keepdims=True)
            variance = jnp.mean(centered * centered, axis=-1, keepdims=True)
            normed = centered * lax.rsqrt(variance + 1e-05) * gain + shift
            columns[at_cols, at_rows, :] = jnp.swapaxes(normed, 0, 1).astype(BF16)
            flat = normed.astype(BF16).reshape(part_rows * width, channels)
            by_row = dot_nt(to_planes, flat)
            stacked = jnp.stack([by_row[:, r * width : (r + 1) * width] for r in range(part_rows)], axis=0)
            planes[:, at_rows, at_cols] = jnp.swapaxes(stacked, 0, 1)[:HEADS].astype(BF16)

        if part == 0:
            pl.semaphore_wait(barrier, len(peers) + 2)
        copy = pltpu.make_async_copy(planes.at[:, at_rows], region(part, 0, 0, every), own_sems.at[part])
        copy.start()
        mine.append(copy)
        near.append((send(part, 0, 0, 0, every, 1), send(part, 0, 1, 0, every, 3)))

    first_cols = first_ref.shape[1]
    blocks = []
    for step in range(1, owners):
        to = (row + step) % owners
        src = columns.at[pl.ds(to * own_cols, first_cols)]
        blocks.append(remote(src, first_ref.at[row], block_send.at[step], block_recv.at[step], (to, col)))
    copy = pltpu.make_async_copy(
        columns.at[pl.ds(row * own_cols, first_cols)], first_ref.at[row], own_sems.at[3]
    )
    copy.start()
    mine.append(copy)
    for owner in range(owners):
        src = columns.at[pl.ds(owner * own_cols + first_cols, own_cols - first_cols)]
        copy = pltpu.make_async_copy(src, later_ref.at[owner], late_sems.at[owner])
        copy.start()
        mine.append(copy)
    for copy in mine[:3]:
        copy.wait()

    copies, pairs = [], []
    for stage in range(3):
        last = stage == 2
        if stage:
            near = []
            for part in range(3):
                near.append((send(part, stage, 0, 0, every, 1), send(part, stage, 1, 0, every, 3)))
                if last:
                    pairs.append(pair(part, 0, 0))
        far = []
        for part in range(3):
            near[part][0].wait_recv()
            near[part][1].wait_recv()
            far.append((send(part, stage, 2, 3, low, 1), send(part, stage, 3, 1, high, 3)))
            if last:
                pairs += [pair(part, 1, 3), pair(part, 2, 1)]
        for part in range(3):
            far[part][0].wait_recv()
            far[part][1].wait_recv()
            if last:
                pairs.append(pair(part, 3, 2))
        copies += [copy for two in near + far for copy in two]
    for copy in copies:
        copy.wait_send()
    for copy in pairs + blocks + mine[3:]:
        copy.wait()


def begin(pair_map, ln_gain, ln_bias, w_bias, owners):
    rows, cols, channels = pair_map.shape
    counts = (SPLIT[0], sum(SPLIT[1:]))
    groups = [jax.ShapeDtypeStruct((owners, count, rows, channels), BF16) for count in counts]
    planes = jax.ShapeDtypeStruct((2, 2, 4, 4, 2, HEADS, rows, cols), BF16)
    vmem, anywhere = pl.BlockSpec(memory_space=pltpu.VMEM), pl.BlockSpec(memory_space=pl.ANY)
    dma = pltpu.SemaphoreType.DMA
    return pl.pallas_call(
        begin_kernel,
        in_specs=[anywhere] + [vmem] * 3,
        out_specs=[anywhere] * 3,
        out_shape=[planes] + groups,
        scratch_shapes=[
            pltpu.VMEM((rows, cols, channels), BF16),
            pltpu.VMEM((cols, rows, channels), BF16),
            pltpu.VMEM((HEADS, rows, cols), BF16),
            dma((3,)),
            dma((4,)),
            dma((owners,)),
            dma((3, 3, 4)),
            dma((3, 3, 4)),
            dma((3, 4)),
            dma((3, 4)),
            dma((owners,)),
            dma((owners,)),
        ],
        compiler_params=pltpu.CompilerParams(
            collective_id=0, has_side_effects=True, vmem_limit_bytes=60 * 2**20
        ),
        name="begin",
    )(pair_map, ln_gain[None], ln_bias[None], w_bias)


def give_back_kernel(mine_ref, got_ref, own_sem, sends, recvs):
    owners = mine_ref.shape[0]
    row, col = lax.axis_index("row"), lax.axis_index("col")
    barrier = pltpu.get_barrier_semaphore()
    peers = [(row + step) % owners for step in range(1, owners)]
    for peer in peers:
        pl.semaphore_signal(barrier, inc=1, device_id=(peer, col), device_id_type=pl.DeviceIdType.MESH)
    own = pltpu.make_async_copy(mine_ref.at[row], got_ref.at[row], own_sem)
    own.start()
    pl.semaphore_wait(barrier, len(peers))
    copies = []
    for step, peer in enumerate(peers):
        copy = pltpu.make_async_remote_copy(
            src_ref=mine_ref.at[peer],
            dst_ref=got_ref.at[row],
            send_sem=sends.at[step],
            recv_sem=recvs.at[step],
            device_id=(peer, col),
            device_id_type=pl.DeviceIdType.MESH,
        )
        copy.start()
        copies.append(copy)
    own.wait()
    for copy in copies:
        copy.wait()


def give_back(update):
    owners = update.shape[0]
    return pl.pallas_call(
        give_back_kernel,
        in_specs=[pl.BlockSpec(memory_space=pl.ANY)],
        out_specs=pl.BlockSpec(memory_space=pl.ANY),
        out_shape=jax.ShapeDtypeStruct(update.shape, BF16),
        scratch_shapes=[
            pltpu.SemaphoreType.DMA,
            pltpu.SemaphoreType.DMA((owners - 1,)),
            pltpu.SemaphoreType.DMA((owners - 1,)),
        ],
        compiler_params=pltpu.CompilerParams(collective_id=1, has_side_effects=True),
        name="give_back",
    )(update)


def attend_kernel(
    tokens_ref, x_ref, planes_ref, real_ref, wq_ref, wk_ref, wv_ref, wg_ref, gate_bias_ref, wo_ref,
    out_ref, bias, keys, values, queries, summed, real, wqg, wv, gate_bias, order, sems,
):
    owners, _, rows, channels = x_ref.shape
    length = owners * rows
    units, per_owner = length // UNIT, rows // UNIT
    chain_units = units // 4
    first = pl.program_id(0) == 0

    def filled(chain):
        def count(unit, total):
            return total + tokens_ref[(chain * chain_units + unit) * UNIT]

        return lax.fori_loop(0, chain_units, count, jnp.int32(0))

    @pl.when(first)
    def _():
        ends = jnp.int32(0)
        for chain in range(4):
            here = filled(chain)

            def note(unit, start, chain=chain):
                order[start + unit] = chain * chain_units + unit
                return start

            lax.fori_loop(0, here, note, ends)
            ends = ends + here
        order[units] = ends

        @pl.loop(ends, units)
        def _(unit):
            order[unit] = 0

    count = order[units]
    tiles = (count + 7) // 8

    def plane_copy(slot):
        unit = order[slot]
        owner = unit // per_owner
        at = pl.ds(pl.multiple_of(unit % per_owner * UNIT, UNIT), UNIT)
        to = pl.ds(pl.multiple_of(slot * UNIT, UNIT), UNIT)
        return pltpu.make_async_copy(
            planes_ref.at[:, :, owner % 4, owner // 8, owner // 4 % 2, :, at, :],
            bias.at[:, :, :, to, :],
            sems.at[slot // 16],
        )

    @pl.when(first)
    def _():
        @pl.loop(0, tiles * 8)
        def _(slot):
            plane_copy(slot).start()

        for slot in range(units):
            unit = order[slot]
            at = pl.ds(pl.multiple_of(unit * UNIT, UNIT), UNIT)
            keep = jnp.where(slot < count, 1.0, 0.0).astype(F32)
            real[slot * UNIT : (slot + 1) * UNIT, :] = (real_ref[at, :].astype(F32) * keep).astype(BF16)
        wqg[:channels] = turned(wq_ref[...])
        wqg[channels:] = turned(wg_ref[...])
        wv[...] = turned(wv_ref[...])
        gate_bias[...] = jnp.transpose(jnp.broadcast_to(gate_bias_ref[...], (channels, channels)))

    x = x_ref[...].reshape(length, channels)
    projected = dot_nt(wqg[...], x)
    queries[...] = (projected[:channels] * (1.0 / math.sqrt(WIDTH))).astype(BF16)
    gate = jax.nn.sigmoid(projected[channels:] + gate_bias[:, :1])
    pieces = []
    for slot in range(units):
        unit = order[slot]
        at = pl.ds(pl.multiple_of(unit % per_owner * UNIT, UNIT), UNIT)
        pieces.append(x_ref[unit // per_owner, 0, at, :])
    compact = jnp.concatenate(pieces, axis=0) * real[...]
    key_all = jnp.dot(compact, wk_ref[...], preferred_element_type=F32).astype(BF16)
    value_all = dot_nt(wv[...], compact).astype(BF16)
    ones = dot_nt(jnp.full((16, channels), 1.0 / channels, BF16), real[...]).astype(BF16)
    for head in range(HEADS):
        lanes = slice(head * WIDTH, (head + 1) * WIDTH)
        keys[head] = key_all[:, lanes]
        values[head, :WIDTH] = value_all[lanes]
        values[head, WIDTH:] = ones

    def arrived(start, count):
        @pl.when(first)
        def _():
            @pl.loop(start, start + count)
            def _(slot):
                plane_copy(slot).wait()

    part_width = length // 4

    def scores(head, at, low, high):
        heads = pl.ds(head * WIDTH, WIDTH)
        raw = jnp.dot(keys[head, at, :], queries[heads, low:high], preferred_element_type=F32)
        added = []
        for part in range(4):
            start, end = max(low - part * part_width, 0), min(high - part * part_width, part_width)
            if start < end:
                added.append(bias[part // 2, part % 2, head, at, start:end])
        return raw + jnp.concatenate(added, axis=1).astype(F32)

    summed[...] = jnp.zeros_like(summed)

    def advance(at, width):
        def add(head, low, weights):
            summed[head, :, low : low + width] += jnp.dot(
                values[head, :, at], weights, preferred_element_type=F32
            )

        pieces = [(head, low) for head in range(HEADS) for low in range(0, length, width)]
        scored, weighted = None, None
        for piece in pieces + [None, None]:
            coming = None
            if piece is not None:
                head, low = piece
                coming = (head, low, scores(head, at, low, low + width))
            ready = None
            if scored is not None:
                ready = (*scored[:2], jnp.exp(scored[2]).astype(BF16))
            if weighted is not None:
                add(*weighted)
            scored, weighted = coming, ready

    wide = tiles // 2

    @pl.loop(0, wide)
    def _(step):
        arrived(step * 16, 16)
        advance(pl.ds(pl.multiple_of(step * 256, 256), 256), 512)

    @pl.when(tiles % 2 == 1)
    def _():
        arrived(wide * 16, 8)
        advance(pl.ds(pl.multiple_of(wide * 256, 256), 128), 768)

    totals = summed[:, WIDTH, :]
    lowest, highest = jnp.min(totals), jnp.max(totals)
    safe = jnp.logical_and(lowest > 2.0**-60, highest < 2.0**100)

    @pl.when(jnp.logical_not(safe))
    def _():
        for head in range(HEADS):

            def masked(step):
                at = pl.ds(pl.multiple_of(step * 128, 128), 128)
                return at, jnp.where(real[at, :1].astype(F32) > 0, scores(head, at, 0, length), -3.0e38)

            def highest_of(step, top):
                return jnp.maximum(top, jnp.max(masked(step)[1], axis=0, keepdims=True))

            top = lax.fori_loop(0, tiles, highest_of, jnp.full((1, length), -3.0e38, F32))
            summed[head] = jnp.zeros_like(summed[head])

            @pl.loop(0, tiles)
            def _(step):
                at, shifted = masked(step)
                weights = jnp.exp(shifted - top).astype(BF16)
                summed[head] += jnp.dot(values[head, :, at], weights, preferred_element_type=F32)

    attended = jnp.concatenate(
        [summed[head, :WIDTH] / summed[head, WIDTH : WIDTH + 1] for head in range(HEADS)], axis=0
    )
    hidden = (gate * attended).astype(BF16)
    update = dot_tn(hidden, wo_ref[...]).astype(BF16)
    out_ref[...] = update.reshape(out_ref.shape)


def attend(x, start, cols, planes, tokens, real, wq, wk, wv, wg, gate_bias, wo):
    owners, _, rows, channels = x.shape
    length = owners * rows
    whole = lambda shape: pl.BlockSpec(shape, lambda j, *_: (0,) * len(shape))
    column = pl.BlockSpec((owners, 1, rows, channels), lambda j, *_: (0, j + start, 0, 0))
    result = pl.BlockSpec((owners, 1, rows, channels), lambda j, *_: (0, j, 0, 0))
    scores = cols * HEADS * length * length
    return pl.pallas_call(
        attend_kernel,
        grid_spec=pltpu.PrefetchScalarGridSpec(
            num_scalar_prefetch=1,
            grid=(cols,),
            in_specs=[
                column,
                pl.BlockSpec(memory_space=pl.ANY),
                whole(real.shape),
                whole(wq.shape),
                whole(wk.shape),
                whole(wv.shape),
                whole(wg.shape),
                whole(gate_bias.shape),
                whole(wo.shape),
            ],
            out_specs=result,
            scratch_shapes=[
                pltpu.VMEM((2, 2, HEADS, length, length // 4), BF16),
                pltpu.VMEM((HEADS, length, WIDTH), BF16),
                pltpu.VMEM((HEADS, WIDTH + 16, length), BF16),
                pltpu.VMEM((channels, length), BF16),
                pltpu.VMEM((HEADS, WIDTH + 16, length), F32),
                pltpu.VMEM((length, channels), BF16),
                pltpu.VMEM((2 * channels, channels), BF16),
                pltpu.VMEM((channels, channels), BF16),
                pltpu.VMEM((channels, channels), F32),
                pltpu.SMEM((length // UNIT + 1,), jnp.int32),
                pltpu.SemaphoreType.DMA((length // (16 * UNIT),)),
            ],
        ),
        out_shape=jax.ShapeDtypeStruct((owners, cols, rows, channels), BF16),
        compiler_params=pltpu.CompilerParams(vmem_limit_bytes=60 * 2**20),
        cost_estimate=pl.CostEstimate(
            flops=scores * 2048, bytes_accessed=planes.size * 2 + x.size * 4, transcendentals=scores
        ),
        name="attend",
    )(tokens, x, planes, real, wq, wk, wv, wg, gate_bias, wo)


def shards(
    pair_map, valid_tokens, ln_gain, ln_bias, w_bias, w_query, w_key, w_value, w_gate, gate_bias, w_out,
):
    rows, cols, channels = pair_map.shape
    owners = lax.axis_size("row")
    length = valid_tokens.shape[0]
    planes, first, later = begin(pair_map, ln_gain, ln_bias, w_bias, owners)
    later = lax.all_to_all(later, "row", split_axis=0, concat_axis=0)
    real = jnp.broadcast_to(valid_tokens[:, None], (length, channels)).astype(BF16)
    arguments = (planes, valid_tokens, real, w_query, w_key, w_value, w_gate, gate_bias[None], w_out)
    returned = []
    source, start = first, 0
    for index, count in enumerate(SPLIT):
        update = attend(source, start, count, *arguments)
        start = start + count if index else 0
        source = later
        if index < len(SPLIT) - 1:
            returned.append(lax.all_to_all(update, "row", split_axis=0, concat_axis=0))
        else:
            returned.append(give_back(update))
    update = jnp.concatenate(returned, axis=1).reshape(cols, rows, channels)
    return jnp.swapaxes(update, 0, 1)


def solution(mesh):
    return jax.shard_map(
        shards,
        mesh=mesh,
        in_specs=(P("row", "col", None), P(), P(), P(), P(), P(), P(), P(), P(), P(), P()),
        out_specs=P("row", "col", None),
        check_vma=False,
    )
```

```python
import math

import jax
import jax.numpy as jnp
from jax import lax
from jax.experimental import pallas as pl
from jax.experimental.pallas import tpu as pltpu
from jax.sharding import PartitionSpec as P

HEADS = 4
WIDTH = 32
SPLIT = (4, 5, 3)
UNIT = 16
F32 = jnp.float32
BF16 = jnp.bfloat16


def dot_nt(a, b):
    return lax.dot_general(a, b, (((1,), (1,)), ((), ())), preferred_element_type=F32)


def dot_tn(a, b):
    return lax.dot_general(a, b, (((0,), (0,)), ((), ())), preferred_element_type=F32)


def turned(matrix):
    return jnp.transpose(matrix.astype(F32)).astype(BF16)


def offsets():
    hops = lambda offset: sum(min(by, 4 - by) for by in offset[:2]) + offset[2]
    every = [(x, y, z) for x in range(4) for y in range(4) for z in range(2) if x or y or z]
    ordered = []
    for offset in sorted(every, key=hops, reverse=True):
        for one in (offset, ((4 - offset[0]) % 4, (4 - offset[1]) % 4, offset[2])):
            if one not in ordered:
                ordered.append(one)
    return ordered


def peers_of(row):
    x, z, y = row % 4, row // 4 % 2, row // 8
    return [((y + dy) % 4 * 2 + (z + dz) % 2) * 4 + (x + dx) % 4 for dx, dy, dz in offsets()]


def begin_kernel(
    pair_hbm, gain_ref, shift_ref, bias_ref, all_ref, first_ref, later_ref,
    pair_ref, columns, planes, in_sems, own_sems, late_sems, send_sems, recv_sems,
    pair_send, pair_recv, block_send, block_recv,
):
    rows, cols, channels = pair_ref.shape
    owners = first_ref.shape[0]
    own_cols = cols // owners
    row, col = lax.axis_index("row"), lax.axis_index("col")
    core = col % 2
    here = {"x": row % 4, "y": row // 8, "z": col // 2 * 2 + row // 4 % 2}
    mesh_ids = pl.DeviceIdType.MESH

    def device(place, on_core):
        return ((place["y"] * 2 + place["z"] % 2) * 4 + place["x"], place["z"] // 2 * 2 + on_core)

    def moved(axis, by):
        return {**here, axis: (here[axis] + by) % 4}

    part_rows = rows // 3
    loads = []
    for part in range(3):
        at_rows = pl.ds(part * part_rows, part_rows)
        copy = pltpu.make_async_copy(pair_hbm.at[at_rows], pair_ref.at[at_rows], in_sems.at[part])
        copy.start()
        loads.append(copy)
    partner = device(here, 1 - core)
    outside = device(moved("z", 3 + 2 * (here["z"] % 2)), core)
    peers = [(peer, col) for peer in peers_of(row)]
    barrier = pltpu.get_barrier_semaphore()
    for friend in peers + [partner, outside]:
        pl.semaphore_signal(barrier, inc=1, device_id=friend, device_id_type=mesh_ids)

    orders = ("zyx", "xzy", "yxz")
    every, low, high = slice(None), pl.ds(0, 2), pl.ds(2, 2)

    def region(part, stage, by, heads):
        place = {}
        for axis in "xyz":
            at = orders[part].index(axis)
            place[axis] = None if at < stage else (here[axis] + by) % 4 if at == stage else here[axis]
        pick = lambda value: slice(None) if value is None else value
        z = place["z"]
        z_hi, z_lo = (None, None) if z is None else (z // 2, z % 2)
        index = (pick(z_hi), core, pick(place["x"]), pick(place["y"]), pick(z_lo), heads)
        return all_ref.at[(*index, pl.ds(part * part_rows, part_rows))]

    def remote(src, dst, sends, recvs, to):
        copy = pltpu.make_async_remote_copy(
            src_ref=src, dst_ref=dst, send_sem=sends, recv_sem=recvs, device_id=to, device_id_type=mesh_ids
        )
        copy.start()
        return copy

    def send(part, stage, kind, by, heads, to):
        ref = region(part, stage, by, heads)
        src = planes.at[:, pl.ds(part * part_rows, part_rows)] if stage == 0 and kind < 2 else ref
        sems = (send_sems.at[part, stage, kind], recv_sems.at[part, stage, kind])
        return remote(src, ref, *sems, device(moved(orders[part][stage], to), core))

    def pair(part, piece, by):
        ref = region(part, 2, by, every)
        return remote(ref, ref, pair_send.at[part, piece], pair_recv.at[part, piece], partner)

    gain, shift = gain_ref[...], shift_ref[...]
    to_planes = jnp.concatenate([bias_ref[...].astype(F32), jnp.zeros((8 - HEADS, channels), F32)], axis=0).astype(BF16)
    width = 128
    mine, near = [], []
    for part in range(3):
        at_rows = slice(part * part_rows, (part + 1) * part_rows)
        loads[part].wait()

        @pl.loop(0, cols // width)
        def _(chunk):
            at_cols = pl.ds(pl.multiple_of(chunk * width, width), width)
            values = pair_ref[at_rows, at_cols, :].astype(F32)
            centered = values - jnp.mean(values, axis=-1, keepdims=True)
            variance = jnp.mean(centered * centered, axis=-1, keepdims=True)
            normed = centered * lax.rsqrt(variance + 1e-05) * gain + shift
            rounded = normed.astype(BF16)
            pair_ref[at_rows, at_cols, :] = rounded
            flat = rounded.reshape(part_rows * width, channels)
            by_row = dot_nt(to_planes, flat)
            stacked = jnp.stack([by_row[:, r * width : (r + 1) * width] for r in range(part_rows)], axis=0)
            planes[:, at_rows, at_cols] = jnp.swapaxes(stacked, 0, 1)[:HEADS].astype(BF16)

        if part == 0:
            pl.semaphore_wait(barrier, len(peers) + 2)
        copy = pltpu.make_async_copy(planes.at[:, at_rows], region(part, 0, 0, every), own_sems.at[part])
        copy.start()
        mine.append(copy)
        near.append((send(part, 0, 0, 0, every, 1), send(part, 0, 1, 0, every, 3)))

    def turn(part):
        at_rows = slice(part * part_rows, (part + 1) * part_rows)

        @pl.loop(0, cols // width)
        def _(chunk):
            at_cols = pl.ds(pl.multiple_of(chunk * width, width), width)
            values = pair_ref[at_rows, at_cols, :].astype(F32)
            columns[at_cols, at_rows, :] = jnp.swapaxes(values, 0, 1).astype(BF16)

    turn(0)
    for copy in mine[:3]:
        copy.wait()

    copies, pairs = [], []
    for stage in range(3):
        last = stage == 2
        if stage:
            near = []
            for part in range(3):
                near.append((send(part, stage, 0, 0, every, 1), send(part, stage, 1, 0, every, 3)))
                if last:
                    pairs.append(pair(part, 0, 0))
        if stage == 1:
            turn(2)
            first_cols = first_ref.shape[1]
            blocks = []
            for step, (to, _) in enumerate(peers):
                src = columns.at[pl.ds(to * own_cols, first_cols)]
                blocks.append(remote(src, first_ref.at[row], block_send.at[step], block_recv.at[step], (to, col)))
            copy = pltpu.make_async_copy(
                columns.at[pl.ds(row * own_cols, first_cols)], first_ref.at[row], own_sems.at[3]
            )
            copy.start()
            mine.append(copy)
            for owner in range(owners):
                src = columns.at[pl.ds(owner * own_cols + first_cols, own_cols - first_cols)]
                copy = pltpu.make_async_copy(src, later_ref.at[owner], late_sems.at[owner])
                copy.start()
                mine.append(copy)
        far = []
        for part in range(3):
            near[part][0].wait_recv()
            near[part][1].wait_recv()
            far.append((send(part, stage, 2, 3, low, 1), send(part, stage, 3, 1, high, 3)))
            if last:
                pairs += [pair(part, 1, 3), pair(part, 2, 1)]
        if stage == 0:
            turn(1)
        for part in range(3):
            far[part][0].wait_recv()
            far[part][1].wait_recv()
            if last:
                pairs.append(pair(part, 3, 2))
        copies += [copy for two in near + far for copy in two]
    for copy in copies:
        copy.wait_send()
    for copy in pairs + blocks + mine[3:]:
        copy.wait()


def begin(pair_map, ln_gain, ln_bias, w_bias, owners):
    rows, cols, channels = pair_map.shape
    counts = (SPLIT[0], sum(SPLIT[1:]))
    groups = [jax.ShapeDtypeStruct((owners, count, rows, channels), BF16) for count in counts]
    planes = jax.ShapeDtypeStruct((2, 2, 4, 4, 2, HEADS, rows, cols), BF16)
    vmem, anywhere = pl.BlockSpec(memory_space=pltpu.VMEM), pl.BlockSpec(memory_space=pl.ANY)
    dma = pltpu.SemaphoreType.DMA
    return pl.pallas_call(
        begin_kernel,
        in_specs=[anywhere] + [vmem] * 3,
        out_specs=[anywhere] * 3,
        out_shape=[planes] + groups,
        scratch_shapes=[
            pltpu.VMEM((rows, cols, channels), BF16),
            pltpu.VMEM((cols, rows, channels), BF16),
            pltpu.VMEM((HEADS, rows, cols), BF16),
            dma((3,)),
            dma((4,)),
            dma((owners,)),
            dma((3, 3, 4)),
            dma((3, 3, 4)),
            dma((3, 4)),
            dma((3, 4)),
            dma((owners,)),
            dma((owners,)),
        ],
        compiler_params=pltpu.CompilerParams(
            collective_id=0, has_side_effects=True, vmem_limit_bytes=60 * 2**20
        ),
        name="begin",
    )(pair_map, ln_gain[None], ln_bias[None], w_bias.T)


def give_back_kernel(mine_ref, got_ref, own_sem, sends, recvs):
    owners = mine_ref.shape[0]
    row, col = lax.axis_index("row"), lax.axis_index("col")
    barrier = pltpu.get_barrier_semaphore()
    peers = peers_of(row)
    for peer in peers:
        pl.semaphore_signal(barrier, inc=1, device_id=(peer, col), device_id_type=pl.DeviceIdType.MESH)
    own = pltpu.make_async_copy(mine_ref.at[row], got_ref.at[row], own_sem)
    own.start()
    pl.semaphore_wait(barrier, len(peers))
    copies = []
    for step, peer in enumerate(peers):
        copy = pltpu.make_async_remote_copy(
            src_ref=mine_ref.at[peer],
            dst_ref=got_ref.at[row],
            send_sem=sends.at[step],
            recv_sem=recvs.at[step],
            device_id=(peer, col),
            device_id_type=pl.DeviceIdType.MESH,
        )
        copy.start()
        copies.append(copy)
    own.wait()
    for copy in copies:
        copy.wait()


def give_back(update):
    owners = update.shape[0]
    return pl.pallas_call(
        give_back_kernel,
        in_specs=[pl.BlockSpec(memory_space=pl.ANY)],
        out_specs=pl.BlockSpec(memory_space=pl.ANY),
        out_shape=jax.ShapeDtypeStruct(update.shape, BF16),
        scratch_shapes=[
            pltpu.SemaphoreType.DMA,
            pltpu.SemaphoreType.DMA((owners - 1,)),
            pltpu.SemaphoreType.DMA((owners - 1,)),
        ],
        compiler_params=pltpu.CompilerParams(collective_id=1, has_side_effects=True),
        name="give_back",
    )(update)


def attend_kernel(
    tokens_ref, x_ref, planes_ref, real_ref, wq_ref, wk_ref, wv_ref, wg_ref, gate_bias_ref, wo_ref,
    out_ref, bias, keys, values, queries, summed, real, wqg, wv, gate_bias, order, sems,
):
    owners, _, rows, channels = x_ref.shape
    length = owners * rows
    units, per_owner = length // UNIT, rows // UNIT
    chain_units = units // 4
    first = pl.program_id(0) == 0

    def filled(chain):
        def count(unit, total):
            return total + tokens_ref[(chain * chain_units + unit) * UNIT]

        return lax.fori_loop(0, chain_units, count, jnp.int32(0))

    @pl.when(first)
    def _():
        ends = jnp.int32(0)
        for chain in range(4):
            here = filled(chain)

            def note(unit, start, chain=chain):
                order[start + unit] = chain * chain_units + unit
                return start

            lax.fori_loop(0, here, note, ends)
            ends = ends + here
        order[units] = ends

        @pl.loop(ends, units)
        def _(unit):
            order[unit] = 0

    count = order[units]
    tiles = (count + 7) // 8

    def plane_copy(slot):
        unit = order[slot]
        owner = unit // per_owner
        at = pl.ds(pl.multiple_of(unit % per_owner * UNIT, UNIT), UNIT)
        to = pl.ds(pl.multiple_of(slot * UNIT, UNIT), UNIT)
        return pltpu.make_async_copy(
            planes_ref.at[:, :, owner % 4, owner // 8, owner // 4 % 2, :, at, :],
            bias.at[:, :, :, to, :],
            sems.at[slot // 16],
        )

    @pl.when(first)
    def _():
        @pl.loop(0, tiles * 8)
        def _(slot):
            plane_copy(slot).start()

        for slot in range(units):
            unit = order[slot]
            at = pl.ds(pl.multiple_of(unit * UNIT, UNIT), UNIT)
            keep = jnp.where(slot < count, 1.0, 0.0).astype(F32)
            real[slot * UNIT : (slot + 1) * UNIT, :] = (real_ref[at, :].astype(F32) * keep).astype(BF16)
        wqg[:channels] = turned(wq_ref[...])
        wqg[channels:] = turned(wg_ref[...])
        wv[...] = turned(wv_ref[...])
        gate_bias[...] = jnp.transpose(jnp.broadcast_to(gate_bias_ref[...], (channels, channels)))

    x = x_ref[...].reshape(length, channels)
    projected = dot_nt(wqg[...], x)
    queries[...] = (projected[:channels] * (1.0 / math.sqrt(WIDTH))).astype(BF16)
    gate = jax.nn.sigmoid(projected[channels:] + gate_bias[:, :1])
    pieces = []
    for slot in range(units):
        unit = order[slot]
        at = pl.ds(pl.multiple_of(unit % per_owner * UNIT, UNIT), UNIT)
        pieces.append(x_ref[unit // per_owner, 0, at, :])
    compact = jnp.concatenate(pieces, axis=0) * real[...]
    key_all = jnp.dot(compact, wk_ref[...], preferred_element_type=F32).astype(BF16)
    value_all = dot_nt(wv[...], compact).astype(BF16)
    ones = dot_nt(jnp.full((16, channels), 1.0 / channels, BF16), real[...]).astype(BF16)
    for head in range(HEADS):
        lanes = slice(head * WIDTH, (head + 1) * WIDTH)
        keys[head] = key_all[:, lanes]
        values[head, :WIDTH] = value_all[lanes]
        values[head, WIDTH:] = ones

    def arrived(start, count):
        @pl.when(first)
        def _():
            @pl.loop(start, start + count)
            def _(slot):
                plane_copy(slot).wait()

    part_width = length // 4

    def scores(head, at, low, high):
        heads = pl.ds(head * WIDTH, WIDTH)
        raw = jnp.dot(keys[head, at, :], queries[heads, low:high], preferred_element_type=F32)
        added = []
        for part in range(4):
            start, end = max(low - part * part_width, 0), min(high - part * part_width, part_width)
            if start < end:
                added.append(bias[part // 2, part % 2, head, at, start:end])
        return raw + jnp.concatenate(added, axis=1).astype(F32)

    summed[...] = jnp.zeros_like(summed)

    def advance(at, width):
        def add(head, low, weights):
            summed[head, :, low : low + width] += jnp.dot(
                values[head, :, at], weights, preferred_element_type=F32
            )

        pieces = [(head, low) for head in range(HEADS) for low in range(0, length, width)]
        scored, weighted = None, None
        for piece in pieces + [None, None]:
            coming = None
            if piece is not None:
                head, low = piece
                coming = (head, low, scores(head, at, low, low + width))
            ready = None
            if scored is not None:
                ready = (*scored[:2], jnp.exp(scored[2]).astype(BF16))
            if weighted is not None:
                add(*weighted)
            scored, weighted = coming, ready

    wide = tiles // 2

    @pl.loop(0, wide)
    def _(step):
        arrived(step * 16, 16)
        advance(pl.ds(pl.multiple_of(step * 256, 256), 256), 512)

    @pl.when(tiles % 2 == 1)
    def _():
        arrived(wide * 16, 8)
        advance(pl.ds(pl.multiple_of(wide * 256, 256), 128), 768)

    totals = summed[:, WIDTH, :]
    lowest, highest = jnp.min(totals), jnp.max(totals)
    safe = jnp.logical_and(lowest > 2.0**-60, highest < 2.0**100)

    @pl.when(jnp.logical_not(safe))
    def _():
        for head in range(HEADS):

            def masked(step):
                at = pl.ds(pl.multiple_of(step * 128, 128), 128)
                return at, jnp.where(real[at, :1].astype(F32) > 0, scores(head, at, 0, length), -3.0e38)

            def highest_of(step, top):
                return jnp.maximum(top, jnp.max(masked(step)[1], axis=0, keepdims=True))

            top = lax.fori_loop(0, tiles, highest_of, jnp.full((1, length), -3.0e38, F32))
            summed[head] = jnp.zeros_like(summed[head])

            @pl.loop(0, tiles)
            def _(step):
                at, shifted = masked(step)
                weights = jnp.exp(shifted - top).astype(BF16)
                summed[head] += jnp.dot(values[head, :, at], weights, preferred_element_type=F32)

    attended = jnp.concatenate(
        [summed[head, :WIDTH] / summed[head, WIDTH : WIDTH + 1] for head in range(HEADS)], axis=0
    )
    hidden = (gate * attended).astype(BF16)
    update = dot_tn(hidden, wo_ref[...]).astype(BF16)
    out_ref[...] = update.reshape(out_ref.shape)


def attend(x, start, cols, planes, tokens, real, wq, wk, wv, wg, gate_bias, wo):
    owners, _, rows, channels = x.shape
    length = owners * rows
    whole = lambda shape: pl.BlockSpec(shape, lambda j, *_: (0,) * len(shape))
    column = pl.BlockSpec((owners, 1, rows, channels), lambda j, *_: (0, j + start, 0, 0))
    result = pl.BlockSpec((owners, 1, rows, channels), lambda j, *_: (0, j, 0, 0))
    scores = cols * HEADS * length * length
    return pl.pallas_call(
        attend_kernel,
        grid_spec=pltpu.PrefetchScalarGridSpec(
            num_scalar_prefetch=1,
            grid=(cols,),
            in_specs=[
                column,
                pl.BlockSpec(memory_space=pl.ANY),
                whole(real.shape),
                whole(wq.shape),
                whole(wk.shape),
                whole(wv.shape),
                whole(wg.shape),
                whole(gate_bias.shape),
                whole(wo.shape),
            ],
            out_specs=result,
            scratch_shapes=[
                pltpu.VMEM((2, 2, HEADS, length, length // 4), BF16),
                pltpu.VMEM((HEADS, length, WIDTH), BF16),
                pltpu.VMEM((HEADS, WIDTH + 16, length), BF16),
                pltpu.VMEM((channels, length), BF16),
                pltpu.VMEM((HEADS, WIDTH + 16, length), F32),
                pltpu.VMEM((length, channels), BF16),
                pltpu.VMEM((2 * channels, channels), BF16),
                pltpu.VMEM((channels, channels), BF16),
                pltpu.VMEM((channels, channels), F32),
                pltpu.SMEM((length // UNIT + 1,), jnp.int32),
                pltpu.SemaphoreType.DMA((length // (16 * UNIT),)),
            ],
        ),
        out_shape=jax.ShapeDtypeStruct((owners, cols, rows, channels), BF16),
        compiler_params=pltpu.CompilerParams(vmem_limit_bytes=60 * 2**20),
        cost_estimate=pl.CostEstimate(
            flops=scores * 2048, bytes_accessed=planes.size * 2 + x.size * 4, transcendentals=scores
        ),
        name="attend",
    )(tokens, x, planes, real, wq, wk, wv, wg, gate_bias, wo)


def shards(
    pair_map, valid_tokens, ln_gain, ln_bias, w_bias, w_query, w_key, w_value, w_gate, gate_bias, w_out,
):
    rows, cols, channels = pair_map.shape
    owners = lax.axis_size("row")
    length = valid_tokens.shape[0]
    planes, first, later = begin(pair_map, ln_gain, ln_bias, w_bias, owners)
    later = lax.all_to_all(later, "row", split_axis=0, concat_axis=0)
    real = jnp.broadcast_to(valid_tokens[:, None], (length, channels)).astype(BF16)
    arguments = (planes, valid_tokens, real, w_query, w_key, w_value, w_gate, gate_bias[None], w_out)
    returned = []
    source, start = first, 0
    for index, count in enumerate(SPLIT):
        update = attend(source, start, count, *arguments)
        start = start + count if index else 0
        source = later
        if index < len(SPLIT) - 1:
            returned.append(lax.all_to_all(update, "row", split_axis=0, concat_axis=0))
        else:
            returned.append(give_back(update))
    update = jnp.concatenate(returned, axis=1).reshape(cols, rows, channels)
    return jnp.swapaxes(update, 0, 1)


def solution(mesh):
    return jax.shard_map(
        shards,
        mesh=mesh,
        in_specs=(P("row", "col", None), P(), P(), P(), P(), P(), P(), P(), P(), P(), P()),
        out_specs=P("row", "col", None),
        check_vma=False,
    )
```
